32 devices in a mesh: groups: 2 (over x), seg: 16 (over z, y, core).
Axes of the slice: x: 2, y: 2, z: 4, core: 2. Of those that a mesh axis runs over, the one named last changes fastest.
Arguments:
- bins: bfloat16 [1024, 128], P(('groups', 'seg')), parts along dimension 0, may hold values from -6 to 6
- conv_weight: bfloat16 [3, 128, 128], replicated, may hold values from -0.3125 to 0.3125
- conv_bias: float32 [128], replicated, may hold values from -3 to 3
- pair_left: bfloat16 [128, 48], replicated, may hold values from -0.5 to 0.5
- pair_right: bfloat16 [128, 48], replicated, may hold values from -0.5 to 0.5
- pair_weight: bfloat16 [3, 3, 48, 48], replicated, may hold values from -0.3125 to 0.3125
- pair_bias: float32 [48], replicated, may hold values from -3 to 3
- head: bfloat16 [48], replicated, may hold values from -0.875 to 0.875
- shifts: int32 [4], replicated, may hold values from -8 to 8, as said below
- flags: int32 [4], replicated, may hold values from 0 to 1, as said below
- dilations: int32 [2], replicated, may hold values from 1 to 4, as said below
Outputs:
- contacts: float32 [1024, 512], P(('groups', 'seg')), parts along dimension 0
The draws below stay inside these ranges and needn't reach their ends.
There are 2 independent parts, one for each index of `groups`. The reference program is written for one: setup_inputs(seed, part) draws one part's arguments, and reference() takes and returns one part's arrays. A program takes and returns all parts, laid end to end along the dimension named above; an argument that names none is the same for every part. Nothing has to cross between parts.
Inputs may be any that keep to these rules, and one draw needn't show every extreme that they name: `shifts`: the largest entry is 8 and the smallest -8. `flags`: exactly half of the views are reverse-complemented. `dilations`: one of the two rates equals 4 and the other is smaller.
All inputs are finite; a program needn't handle non-finite values.
Results may differ from the reference program's by a relative error of at most 0.0055.
Values may be sent and summed in bfloat16 or wider, within the bound.
No kernel may reach another device: no remote copies, remote signals or barrier semaphores. Data moves between devices by JAX's collectives and lax.ppermute only.
A program may use at most 128 MiB of HBM per device.

```python
import jax
import jax.numpy as jnp
from jax import lax

CHANNELS = 128
PAIR_CH = 48
BAND = 512
VIEWS = 4
SHIFT = 8
DMAX = 4
LBINS = 512
HALO = 12


def draw_shifts(key, part):
    first_key, second_key = jax.random.split(jax.random.fold_in(key, 11))
    values = jax.random.randint(first_key, (VIEWS,), -SHIFT, SHIFT + 1)
    order = jax.random.permutation(second_key, VIEWS)
    values = values.at[order[0]].set(SHIFT)
    values = values.at[order[1]].set(-SHIFT)
    return values.astype(jnp.int32)


def draw_flags(key, part):
    order = jax.random.permutation(jax.random.fold_in(key, 23), VIEWS)
    return (order % 2).astype(jnp.int32)


def draw_dilations(key, part):
    first_key, second_key = jax.random.split(jax.random.fold_in(key, 37))
    others = jax.random.randint(first_key, (2,), 1, DMAX)
    which = jax.random.randint(second_key, (), 0, 2)
    return jnp.where(jnp.arange(2) == which, DMAX, others).astype(jnp.int32)


def block_levels(key, dims, cuts, least, top_value):
    def one(dim, parts):
        draws = jax.random.uniform(jax.random.fold_in(jax.random.fold_in(key, 6), dim), (parts,), jnp.float32, least / len(cuts), top_value / len(cuts))
        return jnp.repeat(jnp.exp(draws), dims[dim] // parts).reshape((-1,) + (1,) * (len(dims) - dim - 1))

    gain = one(*cuts[0])
    for cut in cuts[1:]:
        gain = gain * one(*cut)
    return gain


def gaussian(key, extent, scale, bound, cuts=(), kind=jnp.bfloat16):
    result = scale * jax.random.normal(key, extent, jnp.float32)
    if cuts:
        result = result * block_levels(key, extent, cuts, -0.22, 0.18)
    return jnp.clip(result, -bound, bound).astype(kind)


def setup_inputs(seed: int = 0, part: int = 0) -> dict:
    streams_of = jax.random.split(jax.random.key(seed), 12)
    own_keys = jax.random.split(jax.random.fold_in(streams_of[11], part), 12)
    return {
        "bins": gaussian(own_keys[0], (LBINS, CHANNELS), 1.0, 6.0, ((0, 16),)),
        "conv_weight": gaussian(streams_of[1], (3, CHANNELS, CHANNELS), (3 * CHANNELS) ** -0.5, 0.3125),
        "conv_bias": gaussian(streams_of[2], (CHANNELS,), 0.5, 3.0, (), jnp.float32),
        "pair_left": gaussian(streams_of[3], (CHANNELS, PAIR_CH), CHANNELS ** -0.5, 0.5),
        "pair_right": gaussian(streams_of[4], (CHANNELS, PAIR_CH), CHANNELS ** -0.5, 0.5),
        "pair_weight": gaussian(streams_of[5], (3, 3, PAIR_CH, PAIR_CH), (9 * PAIR_CH) ** -0.5, 0.3125),
        "pair_bias": gaussian(streams_of[6], (PAIR_CH,), 0.5, 3.0, (), jnp.float32),
        "head": gaussian(streams_of[7], (PAIR_CH,), PAIR_CH ** -0.5, 0.875),
        "shifts": draw_shifts(jax.random.fold_in(streams_of[11], 71), part),
        "flags": draw_flags(jax.random.fold_in(streams_of[11], 71), part),
        "dilations": draw_dilations(jax.random.fold_in(streams_of[11], 71), part),
    }


block_rows = 256


def view_kernels(conv_weight, flags):
    flipped = conv_weight[::-1, ::-1, :]
    chosen = (flags == 1)[:, None, None, None]
    return jnp.where(chosen, flipped[None], conv_weight[None])


def trunk(source, base, rows, shifts, dilate_seq, kernels, conv_bias, pair_left, pair_right):
    def one_view(shift, kernel):
        start = base + shift
        taps = [lax.dynamic_slice_in_dim(source, start + (tap - 1) * dilate_seq, rows, 0) for tap in range(3)]
        mixed = jnp.zeros((rows, CHANNELS), jnp.float32)
        for tap in range(3):
            mixed = mixed + jnp.dot(taps[tap].astype(jnp.float32), kernel[tap].astype(jnp.float32))
        return taps[1], mixed

    centers, mixed = jax.vmap(one_view)(shifts, kernels)
    feature = (centers.astype(jnp.float32) + jax.nn.relu(mixed + conv_bias)).astype(jnp.bfloat16)
    left = jnp.einsum("vrc,cp->vrp", feature.astype(jnp.float32), pair_left.astype(jnp.float32)).astype(jnp.bfloat16)
    right = jnp.einsum("vrc,cp->vrp", feature.astype(jnp.float32), pair_right.astype(jnp.float32)).astype(jnp.bfloat16)
    return left, right


def pair_block(left_rows, right_rows, first_row, total, dilate_pair, pair_weight, pair_bias, head):
    span = left_rows.shape[1]
    rows_out = span - 2 * DMAX
    width = right_rows.shape[1]
    global_rows = first_row + jnp.arange(span, dtype=jnp.int32)
    offsets = jnp.arange(BAND, dtype=jnp.int32)
    inside = ((global_rows >= 0) & (global_rows < total))[:, None] & ((global_rows[:, None] + offsets[None, :]) < total)
    stacked_weight = pair_weight.reshape(9 * PAIR_CH, PAIR_CH)

    def view_step(view, running):
        left = left_rows[view]
        right_cols = right_rows[view].T
        skewed = jnp.tile(right_cols, (1, span + 1))[:, : span * (width + 1)]
        skewed = skewed.reshape(PAIR_CH, span, width + 1)[:, :, :BAND]
        pairs = jax.nn.relu(left.T.astype(jnp.float32)[:, :, None] + skewed.astype(jnp.float32))
        pairs = jnp.where(inside[None], pairs, 0.0).astype(jnp.bfloat16)
        padded = jnp.pad(pairs, ((0, 0), (0, 0), (DMAX, DMAX)))
        pieces = []
        for row_tap in range(3):
            for col_tap in range(3):
                row_start = (DMAX + (row_tap - 1) * dilate_pair).astype(jnp.int32)
                col_start = (DMAX + (col_tap - 1) * dilate_pair).astype(jnp.int32)
                pieces.append(lax.dynamic_slice(padded, (jnp.int32(0), row_start, col_start), (PAIR_CH, rows_out, BAND)))
        stacked = jnp.concatenate(pieces, 0)
        summed = jnp.einsum("kid,ke->eid", stacked.astype(jnp.float32), stacked_weight.astype(jnp.float32))
        hidden = jax.nn.relu(summed + pair_bias[:, None, None])
        return running + jnp.einsum("eid,e->id", hidden, head.astype(jnp.float32))

    running = lax.fori_loop(0, VIEWS, view_step, jnp.zeros((rows_out, BAND), jnp.float32))
    return running / VIEWS


def reference(bins, conv_weight, conv_bias, pair_left, pair_right, pair_weight, pair_bias, head, shifts, flags, dilations):
    total = bins.shape[0]
    kernels = view_kernels(conv_weight, flags)
    source = jnp.pad(bins, ((HALO, HALO), (0, 0)))
    left, right = trunk(source, HALO, total, shifts, dilations[0], kernels, conv_bias, pair_left, pair_right)
    left_pad = jnp.pad(left, ((0, 0), (DMAX, DMAX), (0, 0)))
    right_pad = jnp.pad(right, ((0, 0), (DMAX, DMAX + BAND), (0, 0)))

    def one_block(number):
        start = number * block_rows
        left_rows = lax.dynamic_slice_in_dim(left_pad, start, block_rows + 2 * DMAX, 1)
        right_rows = lax.dynamic_slice_in_dim(right_pad, start, block_rows + 2 * DMAX + BAND, 1)
        return pair_block(left_rows, right_rows, start - DMAX, total, dilations[1], pair_weight, pair_bias, head)

    blocks = lax.map(one_block, jnp.arange(total // block_rows, dtype=jnp.int32))
    return blocks.reshape(total, BAND)
```

```python
import functools

import jax
import jax.numpy as jnp
from jax import lax
from jax.experimental import pallas as pl
from jax.experimental.pallas import tpu as pltpu
from jax.sharding import PartitionSpec as P

CHANNELS = 128
PAIR_CH = 48
BAND = 512
VIEWS = 4
DMAX = 4
HALO = 12
EDGE = DMAX + HALO
LANES = 128
OUT = -1e30


def taken(tiles, amount):
    lane = lax.broadcasted_iota(jnp.int32, tiles[0].shape, 1)
    turned = [pltpu.roll(tile, (LANES - amount) % LANES, 1) for tile in tiles]
    keep = lane < LANES - amount
    return [
        jnp.where(keep, turned[t], turned[min(t + 1, len(tiles) - 1)]) for t in range(len(tiles))
    ]


def kernel(
    rows,
    total,
    scalars,
    bins,
    conv,
    conv_bias,
    project,
    pair,
    pair_bias,
    head,
    out,
    padded,
    sides,
    pairs,
    found,
):
    reach = rows + 2 * DMAX + 2
    span = -(-(BAND + rows + 2 * EDGE) // 16) * 16
    first = scalars[0]
    seq_rate = scalars[1]
    pair_rate = scalars[2]

    padded[0:EDGE, :] = jnp.zeros((EDGE, CHANNELS), jnp.float32)
    padded[EDGE : EDGE + total, :] = bins[...].astype(jnp.float32)
    padded[EDGE + total :, :] = jnp.zeros(
        (padded.shape[0] - EDGE - total, CHANNELS), jnp.float32
    )
    taps = [
        padded[pl.ds(first + DMAX + (tap - 1) * seq_rate, span), :] for tap in range(3)
    ]
    stacked = jnp.concatenate([tap.astype(jnp.bfloat16) for tap in taps], 1)
    mixed = jnp.dot(stacked, conv[...], preferred_element_type=jnp.float32)
    for flag in range(2):
        part = mixed[:, flag * CHANNELS : (flag + 1) * CHANNELS]
        feature = (taps[1] + jnp.maximum(part + conv_bias[...], 0.0)).astype(jnp.bfloat16)
        both = lax.dot_general(
            project[...], feature, (((1,), (1,)), ((), ())), preferred_element_type=jnp.float32
        )
        sides[flag, :, 0:span] = both.astype(jnp.bfloat16).astype(jnp.float32)

    width = sides.shape[2]

    def prepare(view, carry):
        shift = scalars[3 + view]
        flag = scalars[3 + VIEWS + view]
        both = sides[flag]
        moved = taken(
            [both[:, t * LANES : (t + 1) * LANES] for t in range(width // LANES)],
            shift + HALO - DMAX,
        )
        lane = lax.broadcasted_iota(jnp.int32, (PAIR_CH, LANES), 1)
        place = first - DMAX + lane
        left = jnp.where((place >= 0) & (place < total), moved[0][:PAIR_CH], OUT)
        right = jnp.concatenate(
            [
                jnp.where(place + t * LANES < total, moved[t][PAIR_CH:], OUT)
                for t in range(width // LANES)
            ],
            1,
        )
        for row in range(reach):
            value = left[:, row : row + 1] + right[:, row : row + BAND]
            pairs[view, row] = jnp.maximum(value, 0.0).astype(jnp.bfloat16)
        return carry

    lax.fori_loop(0, VIEWS, prepare, 0)

    lane = lax.broadcasted_iota(jnp.int32, (PAIR_CH, LANES), 1)
    tiles = BAND // LANES

    def group(number, carry):
        block = lax.div(number, pair_rate)
        base = number + block * pair_rate
        sums = [[None] * tiles for _ in range(2)]
        for view in range(VIEWS):
            stack = jnp.concatenate(
                [pairs[view, base + DMAX + (cell - 1) * pair_rate] for cell in range(4)], 0
            )
            product = jnp.dot(pair[...], stack, preferred_element_type=jnp.float32)
            for half in range(2):
                low, mid, high = [
                    product[(3 * half + tap) * PAIR_CH : (3 * half + tap + 1) * PAIR_CH]
                    for tap in range(3)
                ]
                up = [
                    pltpu.roll(low[:, t * LANES : (t + 1) * LANES], pair_rate, 1)
                    for t in range(tiles)
                ]
                down = [
                    pltpu.roll(high[:, t * LANES : (t + 1) * LANES], LANES - pair_rate, 1)
                    for t in range(tiles)
                ]
                for t in range(tiles):
                    before = up[t - 1] if t else 0.0
                    after = down[t + 1] if t + 1 < tiles else 0.0
                    value = (
                        mid[:, t * LANES : (t + 1) * LANES]
                        + jnp.where(lane < pair_rate, before, up[t])
                        + jnp.where(lane >= LANES - pair_rate, after, down[t])
                    )
                    hidden = jnp.maximum(value + pair_bias[...], 0.0)
                    sums[half][t] = hidden if view == 0 else sums[half][t] + hidden
        for half in range(2):
            row = jnp.concatenate(
                [
                    jnp.sum(sums[half][t] * head[...], axis=0, keepdims=True)
                    for t in range(tiles)
                ],
                1,
            )
            found[pl.ds(base + half * pair_rate, 1), :] = row * (1.0 / VIEWS)
        return carry

    blocks = rows // (2 * pair_rate)
    left_over = rows - blocks * 2 * pair_rate
    groups = blocks * pair_rate + jnp.minimum(left_over, pair_rate)
    lax.fori_loop(0, groups, group, 0)
    out[...] = found[0:rows, :]


def per_device(
    bins,
    conv_weight,
    conv_bias,
    pair_left,
    pair_right,
    pair_weight,
    pair_bias,
    head,
    shifts,
    flags,
    dilations,
):
    rows = bins.shape[0]
    segments = lax.axis_size("seg")
    total = rows * segments
    first = lax.axis_index("seg") * rows
    every = lax.all_to_all(
        jnp.broadcast_to(bins[None], (segments,) + bins.shape), "seg", 0, 0
    ).reshape(total, CHANNELS)
    taps = conv_weight.reshape(3 * CHANNELS, CHANNELS)
    conv = jnp.concatenate([taps, taps[::-1]], 1)
    project = jnp.concatenate([pair_left, pair_right], 1).T
    by_out = pair_weight.transpose(1, 3, 0, 2).reshape(3 * PAIR_CH, 3 * PAIR_CH)
    pair = jnp.concatenate(
        [
            jnp.pad(by_out, ((0, 0), (0, PAIR_CH))),
            jnp.pad(by_out, ((0, 0), (PAIR_CH, 0))),
        ],
        0,
    )
    scalars = jnp.concatenate([first[None], dilations, shifts, flags]).astype(jnp.int32)
    span = -(-(BAND + rows + 2 * EDGE) // 16) * 16
    width = -(-span // LANES) * LANES
    whole = pl.BlockSpec(memory_space=pltpu.VMEM)
    return pl.pallas_call(
        functools.partial(kernel, rows, total),
        out_shape=jax.ShapeDtypeStruct((rows, BAND), jnp.float32),
        in_specs=[pl.BlockSpec(memory_space=pltpu.SMEM)] + [whole] * 7,
        out_specs=whole,
        scratch_shapes=[
            pltpu.VMEM((total + span + EDGE, CHANNELS), jnp.float32),
            pltpu.VMEM((2, 2 * PAIR_CH, width), jnp.float32),
            pltpu.VMEM((VIEWS, rows + 2 * DMAX + 2, PAIR_CH, BAND), jnp.bfloat16),
            pltpu.VMEM((rows + DMAX + 4, BAND), jnp.float32),
        ],
        compiler_params=pltpu.CompilerParams(vmem_limit_bytes=40 << 20),
    )(
        scalars,
        every,
        conv,
        conv_bias[None],
        project,
        pair,
        jnp.broadcast_to(pair_bias[:, None], (PAIR_CH, LANES)),
        jnp.broadcast_to(head.astype(jnp.float32)[:, None], (PAIR_CH, LANES)),
    )


def solution(mesh):
    placed = (P(("groups", "seg"), None), P(), P(), P(), P(), P(), P(), P(), P(), P(), P())
    return jax.shard_map(
        per_device,
        mesh=mesh,
        in_specs=placed,
        out_specs=P(("groups", "seg"), None),
        check_vma=False,
    )
```

```python
import functools

import jax
import jax.numpy as jnp
from jax import lax
from jax.experimental import pallas as pl
from jax.experimental.pallas import tpu as pltpu
from jax.sharding import PartitionSpec as P

CHANNELS = 128
PAIR_CH = 48
BAND = 512
VIEWS = 4
DMAX = 4
HALO = 20
EDGE = DMAX + HALO
LANES = 128
OUT = -1e30
STEPS = 6


def rounds(segments):
    chips = segments // 2
    return [(max(m, 1), m + 1) for m in range(0, chips, 2)]


def taken(tiles, amount):
    lane = lax.broadcasted_iota(jnp.int32, tiles[0].shape, 1)
    turned = [pltpu.roll(tile, (LANES - amount) % LANES, 1) for tile in tiles]
    keep = lane < LANES - amount
    return [
        jnp.where(keep, turned[t], turned[min(t + 1, len(tiles) - 1)]) for t in range(len(tiles))
    ]


def kernel(
    rows,
    total,
    *refs,
):
    (near, far, across_far, conv, project, pair, floor, head, conv_bias, numbers) = refs[:10]
    (out, padded, sides, lefts, rights, floors, found) = refs[10:17]
    shifts = [numbers[0, place] for place in range(VIEWS)]
    flags = [numbers[0, VIEWS + place] for place in range(VIEWS)]
    dilations = [numbers[0, 2 * VIEWS + place] for place in range(2)]
    reach = rows + 2 * DMAX + 4
    span = -(-(BAND + rows + 2 * EDGE) // 16) * 16
    first = lax.axis_index("seg") * rows
    seq_rate = dilations[0]
    pair_rate = dilations[1]

    padded[0:EDGE, :] = jnp.zeros((EDGE, CHANNELS), jnp.float32)
    padded[EDGE + total :, :] = jnp.zeros(
        (padded.shape[0] - EDGE - total, CHANNELS), jnp.float32
    )
    me = lax.div(first, rows)
    pieces = [(near, 0, me)]
    for turn, masks in enumerate(rounds(total // rows)):
        even = lax.rem(me, 2) == 0
        ours = jnp.where(even, masks[0], masks[1])
        theirs = jnp.where(even, masks[1], masks[0])
        pieces.append((far, 2 * rows * turn, lax.bitwise_xor(me, 2 * ours)))
        pieces.append(
            (across_far, 2 * rows * turn, lax.bitwise_xor(lax.bitwise_xor(me, 1), 2 * theirs))
        )
    for ref, start, segment in pieces:
        for core in range(2):
            place = lax.bitwise_xor(segment, core) * rows
            padded[pl.ds(pl.multiple_of(EDGE + place, 8), rows), :] = ref[
                start + core * rows : start + (core + 1) * rows, :
            ].astype(jnp.float32)
    taps = [
        padded[pl.ds(first + DMAX + (tap - 1) * seq_rate, span), :] for tap in range(3)
    ]
    stacked = jnp.concatenate([tap.astype(jnp.bfloat16) for tap in taps], 1)
    mixed = jnp.dot(stacked, conv[...], preferred_element_type=jnp.float32)
    for flag in range(2):
        part = mixed[:, flag * CHANNELS : (flag + 1) * CHANNELS]
        feature = (taps[1] + jnp.maximum(part + conv_bias[...], 0.0)).astype(jnp.bfloat16)
        both = lax.dot_general(
            project[...], feature, (((1,), (1,)), ((), ())), preferred_element_type=jnp.float32
        )
        sides[flag, :, span:] = jnp.zeros((2 * PAIR_CH, sides.shape[2] - span), jnp.float32)
        sides[flag, :, 0:span] = both.astype(jnp.bfloat16).astype(jnp.float32)

    width = sides.shape[2]
    tiles = BAND // LANES
    lane = lax.broadcasted_iota(jnp.int32, (PAIR_CH, LANES), 1)

    def prepare(view):
        shift = shifts[view]
        flag = flags[view]
        both = sides[flag]
        cut = [both[:, t * LANES : (t + 1) * LANES] for t in range(width // LANES)]
        left = taken([c[:PAIR_CH] for c in cut[:2]], shift + HALO - DMAX)[0]
        place = first - DMAX + lane
        left = jnp.where((place >= 0) & (place < total), left, 0.0)
        turned = [left] + [pltpu.roll(left, LANES - by * pair_rate, 1) for by in (1, 2)]
        level = [
            pltpu.roll(value, (LANES + pair_rate - DMAX) % LANES, 1).astype(jnp.bfloat16)
            for value in turned
        ]
        spread = jnp.concatenate([value for value in level for _ in range(3)], 0)
        floors[view] = floor[...] - jnp.dot(
            pair[0:PAIR_CH, 0 : 9 * PAIR_CH], spread, preferred_element_type=jnp.float32
        )
        left = -left.astype(jnp.bfloat16)
        for row in range(reach):
            lefts[view, row] = jnp.broadcast_to(left[:, row : row + 1], (PAIR_CH, LANES))
        rights[view, STEPS] = jnp.full((PAIR_CH, width), OUT, jnp.bfloat16)
        for step in range(STEPS):
            offset = (step - 2) * pair_rate
            right = taken([c[PAIR_CH:] for c in cut], shift + HALO + offset)
            for t in range(width // LANES):
                rights[view, step, :, t * LANES : (t + 1) * LANES] = jnp.where(
                    first + offset + t * LANES + lane < total, right[t], OUT
                ).astype(jnp.bfloat16)

    for view in range(VIEWS):
        prepare(view)

    def group(number):
        block = lax.div(number, pair_rate)
        base = number + block * pair_rate
        sums = [[0.0] * tiles for _ in range(2)]
        offsets = [0.0, 0.0]
        wrapped = lane < base
        caps = [
            jnp.where(gone, OUT, -OUT).astype(jnp.bfloat16)
            for gone in (
                (lane >= base) & (lane < base + pair_rate),
                (lane >= base - pair_rate) & (lane < base),
                lane >= base - pair_rate + LANES,
            )
        ]
        for view in range(VIEWS):
            sides_of = [
                lefts[view, base + DMAX + (cell - 1) * pair_rate] for cell in range(4)
            ]
            kept = []
            for cell in range(4):
                place = first + base + (cell - 1) * pair_rate
                kept.append((place >= 0) & (place < total))
            lows = []
            for half in range(2):
                turned = pltpu.roll(floors[view], LANES - base - half * pair_rate, 1)
                lows.append(jnp.broadcast_to(turned[:, 0:1], (PAIR_CH, LANES)))
                for e in range(0, PAIR_CH, 8):
                    offsets[half] = offsets[half] + lows[half][e : e + 8] * head[e : e + 8, :]
            for wide in range(tiles // 2):
                chosen = (2 * wide, 2 * wide + 1)
                cells = []
                for cell in range(4):
                    for tap in range(3):
                        step = jnp.where(kept[cell], cell + tap, STEPS)
                        row = [
                            rights[view, step, :, t * LANES : (t + 1) * LANES] for t in chosen
                        ]
                        if wide == 0:
                            last = rights[view, step, :, tiles * LANES :]
                            row[0] = jnp.where(wrapped, last, row[0])
                        if wide == 0 and tap == 0:
                            row[0] = jnp.minimum(row[0], caps[0])
                        if wide == 0 and tap == 2:
                            row[0] = jnp.minimum(row[0], caps[1])
                        if wide == 1 and tap == 2:
                            row[1] = jnp.minimum(row[1], caps[2])
                        cells.append(
                            jnp.concatenate([jnp.maximum(r, sides_of[cell]) for r in row], 1)
                        )
                stack = jnp.concatenate(cells, 0)
                product = jnp.dot(pair[...], stack, preferred_element_type=jnp.float32)
                for half in range(2):
                    for t in chosen:
                        for e in range(0, PAIR_CH, 8):
                            part = product[
                                half * PAIR_CH + e : half * PAIR_CH + e + 8,
                                (t - chosen[0]) * LANES : (t - chosen[0] + 1) * LANES,
                            ]
                            sums[half][t] = (
                                sums[half][t]
                                + jnp.maximum(part, lows[half][e : e + 8]) * head[e : e + 8, :]
                            )
        sums = [[sums[half][t] - offsets[half] for t in range(tiles)] for half in range(2)]
        for half in range(2):
            found[base + half * pair_rate] = jnp.concatenate(sums[half], 1)

    def groups_of_two(number, carry):
        group(2 * number)
        group(2 * number + 1)
        return carry

    blocks = lax.div(rows + 2 * pair_rate - 1, 2 * pair_rate)
    lax.fori_loop(0, lax.div(blocks * pair_rate, 2), groups_of_two, 0)

    lane1 = lane[:1]
    for place in range(rows):
        block = lax.div(place, 2 * pair_rate)
        base = block * 2 * pair_rate + lax.rem(place - block * 2 * pair_rate, pair_rate)
        row = jnp.sum(found[place], axis=0, keepdims=True) * (1.0 / VIEWS)
        turned = [
            pltpu.roll(row[:, t * LANES : (t + 1) * LANES], lax.rem(LANES - base, LANES), 1)
            for t in range(tiles)
        ]
        out[place : place + 1, :] = jnp.concatenate(
            [
                jnp.where(lane1 < LANES - base, turned[t], turned[(t + 1) % tiles])
                for t in range(tiles)
            ],
            1,
        )


def weights_kernel(
    conv_weight,
    pair_left,
    pair_right,
    pair_weight,
    pair_bias,
    head,
    conv_bias,
    shifts,
    flags,
    dilations,
    conv,
    project,
    pair,
    floor,
    out_head,
    out_bias,
    out_numbers,
    wide,
):
    row = lax.broadcasted_iota(jnp.int32, (CHANNELS, CHANNELS), 0)
    column = lax.broadcasted_iota(jnp.int32, (CHANNELS, CHANNELS), 1)
    turn = (row + column == CHANNELS - 1).astype(jnp.float32).astype(jnp.bfloat16)
    for tap in range(3):
        here = slice(tap * CHANNELS, (tap + 1) * CHANNELS)
        there = slice((2 - tap) * CHANNELS, (3 - tap) * CHANNELS)
        conv[here, 0:CHANNELS] = conv_weight[here, :]
        conv[here, CHANNELS:] = jnp.dot(
            turn, conv_weight[there, :], preferred_element_type=jnp.float32
        ).astype(jnp.bfloat16)
    project[0:PAIR_CH, :] = pair_left[...]
    project[PAIR_CH:, :] = pair_right[...]
    taps = 9 * PAIR_CH
    wide[...] = jnp.zeros(wide.shape, jnp.float32)
    turned = pair_weight[...].astype(jnp.float32).T
    wide[0:PAIR_CH, 0:taps] = turned
    wide[PAIR_CH:, taps // 3 : taps // 3 + taps] = turned
    pair[...] = wide[...].astype(jnp.bfloat16)
    floor[...] = -jnp.broadcast_to(pair_bias[...], (LANES, PAIR_CH)).T
    out_bias[...] = conv_bias[...]
    out_numbers[:, 0:VIEWS] = shifts[...]
    out_numbers[:, VIEWS : 2 * VIEWS] = flags[...]
    out_numbers[:, 2 * VIEWS :] = dilations[...]
    out_head[...] = jnp.broadcast_to(head[...].astype(jnp.float32), (LANES, PAIR_CH)).T


def prepared(
    conv_weight,
    pair_left,
    pair_right,
    pair_weight,
    pair_bias,
    head,
    conv_bias,
    shifts,
    flags,
    dilations,
):
    whole = pl.BlockSpec(memory_space=pltpu.VMEM)
    made = [
        ((3 * CHANNELS, 2 * CHANNELS), jnp.bfloat16),
        ((2 * PAIR_CH, CHANNELS), jnp.bfloat16),
        ((2 * PAIR_CH, 12 * PAIR_CH), jnp.bfloat16),
        ((PAIR_CH, LANES), jnp.float32),
        ((PAIR_CH, LANES), jnp.float32),
        ((1, CHANNELS), jnp.float32),
        ((1, 2 * VIEWS + 2), jnp.int32),
    ]
    return pl.pallas_call(
        weights_kernel,
        out_shape=[pltpu.VMEM(*one) for one in made],
        in_specs=[whole] * 10,
        out_specs=[whole] * 7,
        scratch_shapes=[pltpu.VMEM((2 * PAIR_CH, 12 * PAIR_CH), jnp.float32)],
        cost_estimate=pl.CostEstimate(flops=10**9, bytes_accessed=10**6, transcendentals=0),
    )(
        conv_weight.reshape(3 * CHANNELS, CHANNELS),
        pair_left.T,
        pair_right.T,
        pair_weight.reshape(9 * PAIR_CH, PAIR_CH),
        pair_bias[None],
        head[None],
        conv_bias[None],
        shifts[None],
        flags[None],
        dilations[None],
    )


def main_call(rows, total, near, far, across_far, weights):
    span = -(-(BAND + rows + 2 * EDGE) // 16) * 16
    width = -(-span // LANES) * LANES
    whole = pl.BlockSpec(memory_space=pltpu.VMEM)
    return pl.pallas_call(
        functools.partial(kernel, rows, total),
        out_shape=jax.ShapeDtypeStruct((rows, BAND), jnp.float32),
        in_specs=[whole] * 10,
        out_specs=whole,
        scratch_shapes=[
            pltpu.VMEM((total + span + EDGE, CHANNELS), jnp.float32),
            pltpu.VMEM((2, 2 * PAIR_CH, width), jnp.float32),
            pltpu.VMEM((VIEWS, rows + 2 * DMAX + 4, PAIR_CH, LANES), jnp.bfloat16),
            pltpu.VMEM((VIEWS, STEPS + 1, PAIR_CH, width), jnp.bfloat16),
            pltpu.VMEM((VIEWS, PAIR_CH, LANES), jnp.float32),
            pltpu.VMEM((rows + 2 * DMAX, 8, BAND), jnp.float32),
        ],
        compiler_params=pltpu.CompilerParams(vmem_limit_bytes=40 << 20),
    )(near, far, across_far, *weights)


def per_device(
    bins,
    conv_weight,
    conv_bias,
    pair_left,
    pair_right,
    pair_weight,
    pair_bias,
    head,
    shifts,
    flags,
    dilations,
):
    rows = bins.shape[0]
    segments = lax.axis_size("seg")

    def exchanged(value, masks):
        route = [(i, i ^ masks[i % 2]) for i in range(segments)]
        return lax.ppermute(value, "seg", route)

    near = jnp.concatenate([bins, exchanged(bins, (1, 1))], 0)
    parts = [exchanged(near, (2 * even, 2 * odd)) for even, odd in rounds(segments)]
    weights = prepared(
        conv_weight,
        pair_left,
        pair_right,
        pair_weight,
        pair_bias,
        head,
        conv_bias,
        shifts,
        flags,
        dilations,
    )
    parts, weights = lax.optimization_barrier((parts, weights))
    far = jnp.concatenate(parts, 0)
    across_far = exchanged(far, (1, 1))
    return main_call(rows, rows * segments, near, far, across_far, weights)


def solution(mesh):
    placed = (P(("groups", "seg"), None), P(), P(), P(), P(), P(), P(), P(), P(), P(), P())
    return jax.shard_map(
        per_device,
        mesh=mesh,
        in_specs=placed,
        out_specs=P(("groups", "seg"), None),
        check_vma=False,
    )
```

```python
import functools

import jax
import jax.numpy as jnp
from jax import lax
from jax.experimental import pallas as pl
from jax.experimental.pallas import tpu as pltpu
from jax.sharding import PartitionSpec as P

CHANNELS = 128
PAIR_CH = 48
BAND = 512
VIEWS = 4
DMAX = 4
HALO = 20
EDGE = DMAX + HALO
LANES = 128
OUT = -1e30
PACK = 3
SPREAD = 64
CELLS = PACK + 2
STEPS = PACK + 4


def rounds(segments):
    chips = segments // 2
    return [(max(m, 1), m + 1) for m in range(0, chips, 2)]


def taken(tiles, amount):
    lane = lax.broadcasted_iota(jnp.int32, tiles[0].shape, 1)
    turned = [pltpu.roll(tile, (LANES - amount) % LANES, 1) for tile in tiles]
    keep = lane < LANES - amount
    return [
        jnp.where(keep, turned[t], turned[min(t + 1, len(tiles) - 1)]) for t in range(len(tiles))
    ]


def kernel(
    rows,
    total,
    *refs,
):
    (near, far, across_far, conv, project, pair, floor, head, conv_bias, numbers, ones) = refs[:11]
    (out, padded, sides, lefts, rights, floors, found) = refs[11:18]
    shifts = [numbers[0, place] for place in range(VIEWS)]
    flags = [numbers[0, VIEWS + place] for place in range(VIEWS)]
    dilations = [numbers[0, 2 * VIEWS + place] for place in range(2)]
    reach = rows + 3 * DMAX
    span = -(-(BAND + rows + 2 * EDGE) // 16) * 16
    first = lax.axis_index("seg") * rows
    seq_rate = dilations[0]
    pair_rate = dilations[1]

    padded[0:EDGE, :] = jnp.zeros((EDGE, CHANNELS), jnp.float32)
    padded[EDGE + total :, :] = jnp.zeros(
        (padded.shape[0] - EDGE - total, CHANNELS), jnp.float32
    )
    me = lax.div(first, rows)
    pieces = [(near, 0, me)]
    for turn, masks in enumerate(rounds(total // rows)):
        even = lax.rem(me, 2) == 0
        ours = jnp.where(even, masks[0], masks[1])
        theirs = jnp.where(even, masks[1], masks[0])
        pieces.append((far, 2 * rows * turn, lax.bitwise_xor(me, 2 * ours)))
        pieces.append(
            (across_far, 2 * rows * turn, lax.bitwise_xor(lax.bitwise_xor(me, 1), 2 * theirs))
        )
    for ref, start, segment in pieces:
        for core in range(2):
            place = lax.bitwise_xor(segment, core) * rows
            padded[pl.ds(pl.multiple_of(EDGE + place, 8), rows), :] = ref[
                start + core * rows : start + (core + 1) * rows, :
            ].astype(jnp.float32)
    taps = [
        padded[pl.ds(first + DMAX + (tap - 1) * seq_rate, span), :] for tap in range(3)
    ]
    stacked = jnp.concatenate([tap.astype(jnp.bfloat16) for tap in taps], 1)
    mixed = jnp.dot(stacked, conv[...], preferred_element_type=jnp.float32)
    for flag in range(2):
        part = mixed[:, flag * CHANNELS : (flag + 1) * CHANNELS]
        feature = (taps[1] + jnp.maximum(part + conv_bias[...], 0.0)).astype(jnp.bfloat16)
        both = lax.dot_general(
            project[...], feature, (((1,), (1,)), ((), ())), preferred_element_type=jnp.float32
        )
        sides[flag, :, span:] = jnp.zeros((2 * PAIR_CH, sides.shape[2] - span), jnp.bfloat16)
        sides[flag, :, 0:span] = both.astype(jnp.bfloat16)

    width = sides.shape[2]
    tiles = BAND // LANES
    lane = lax.broadcasted_iota(jnp.int32, (PAIR_CH, LANES), 1)

    def prepare(view):
        shift = shifts[view]
        flag = flags[view]
        both = sides[flag]
        cut = [both[:, t * LANES : (t + 1) * LANES] for t in range(width // LANES)]
        left = taken([c[:PAIR_CH] for c in cut[:2]], shift + HALO - DMAX)[0]
        place = first - DMAX + lane
        left = jnp.where((place >= 0) & (place < total), left, 0.0).astype(jnp.bfloat16)
        turned = [left] + [pltpu.roll(left, LANES - by * pair_rate, 1) for by in (1, 2)]
        level = [
            pltpu.roll(value, (LANES + pair_rate - DMAX) % LANES, 1)
            for value in turned
        ]
        spread = jnp.concatenate([value for value in level for _ in range(3)], 0)
        low = floor[...] - jnp.dot(
            pair[0:PAIR_CH, 0 : 9 * PAIR_CH], spread, preferred_element_type=jnp.float32
        )
        high = low.astype(jnp.bfloat16)
        rest = (low - high.astype(jnp.float32)).astype(jnp.bfloat16)
        lows_of.append(jnp.concatenate([high[:, 0:SPREAD], rest[:, 0:SPREAD]], 1))
        rows_of.append(-left[:, 0:SPREAD])
        rights[view, STEPS] = jnp.full((PAIR_CH, width), OUT, jnp.bfloat16)
        for step in range(STEPS):
            offset = (step - 3) * pair_rate
            right = taken([c[PAIR_CH:] for c in cut], shift + HALO + offset)
            for t in range(width // LANES):
                rights[view, step, :, t * LANES : (t + 1) * LANES] = jnp.where(
                    first + offset + t * LANES + lane < total, right[t], OUT
                ).astype(jnp.bfloat16)

    rows_of = []
    lows_of = []
    for view in range(VIEWS):
        prepare(view)
    stacked = jnp.concatenate(rows_of, 0)
    for row in range(0, reach, 4):
        spread = jnp.dot(
            stacked,
            ones[0:SPREAD, row * LANES : (row + 4) * LANES],
            preferred_element_type=jnp.float32
        ).astype(jnp.bfloat16)
        for view in range(VIEWS):
            for which in range(4):
                lefts[view, row + which] = spread[
                    view * PAIR_CH : (view + 1) * PAIR_CH, which * LANES : (which + 1) * LANES
                ]

    stacked = jnp.concatenate(lows_of, 0)
    for row in range(0, rows + 2 * DMAX, 4):
        spread = jnp.dot(
            stacked, ones[:, row * LANES : (row + 4) * LANES], preferred_element_type=jnp.float32
        )
        for view in range(VIEWS):
            for which in range(4):
                floors[view, row + which] = spread[
                    view * PAIR_CH : (view + 1) * PAIR_CH, which * LANES : (which + 1) * LANES
                ]

    def group(number):
        block = lax.div(number, pair_rate)
        base = number + block * (PACK - 1) * pair_rate
        sums = [[0.0] * tiles for _ in range(PACK)]
        offsets = [0.0] * PACK
        seam = base + pair_rate
        wrapped = lane < seam
        caps = [
            jnp.where(gone, OUT, -OUT).astype(jnp.bfloat16)
            for gone in (
                (lane >= seam) & (lane < seam + pair_rate),
                (lane >= base) & (lane < seam),
            )
        ]
        for view in range(VIEWS):
            sides_of = [
                lefts[view, base + DMAX + (cell - 1) * pair_rate] for cell in range(CELLS)
            ]
            above = first + base < pair_rate
            lows = []
            for half in range(PACK):
                lows.append(floors[view, base + half * pair_rate])
                for e in range(0, PAIR_CH, 8):
                    offsets[half] = offsets[half] + lows[half][e : e + 8] * head[e : e + 8, :]
            for wide in range(tiles // 2):
                chosen = (2 * wide, 2 * wide + 1)
                across = {}
                for step in range(-3, STEPS):
                    at = step if step >= 0 else jnp.where(above, STEPS, step + 3)
                    row = [rights[view, at, :, t * LANES : (t + 1) * LANES] for t in chosen]
                    if wide == 0:
                        last = rights[view, at, :, tiles * LANES :]
                        row[0] = jnp.where(wrapped, last, row[0])
                    across[step] = row
                cells = []
                for cell in range(CELLS):
                    for tap in range(3):
                        row = list(across[cell + tap if cell else tap - 3])
                        if wide == 0 and tap == 0:
                            row[0] = jnp.minimum(row[0], caps[0])
                        if wide == 0 and tap == 2:
                            row[0] = jnp.minimum(row[0], caps[1])
                        cells.append(
                            jnp.concatenate([jnp.maximum(r, sides_of[cell]) for r in row], 1)
                        )
                stack = jnp.concatenate(cells, 0)
                product = jnp.dot(pair[...], stack, preferred_element_type=jnp.float32)
                for half in range(PACK):
                    for t in chosen:
                        for e in range(0, PAIR_CH, 8):
                            part = product[
                                half * PAIR_CH + e : half * PAIR_CH + e + 8,
                                (t - chosen[0]) * LANES : (t - chosen[0] + 1) * LANES,
                            ]
                            sums[half][t] = (
                                sums[half][t]
                                + jnp.maximum(part, lows[half][e : e + 8]) * head[e : e + 8, :]
                            )
        sums = [[sums[half][t] - offsets[half] for t in range(tiles)] for half in range(PACK)]
        for half in range(PACK):
            found[base + half * pair_rate] = jnp.concatenate(sums[half], 1)

    def groups_of_two(number, carry):
        group(2 * number)
        group(2 * number + 1)
        return carry

    deep = PACK * pair_rate
    groups = lax.div(rows + deep - 1, deep) * pair_rate
    lax.fori_loop(0, lax.div(groups + 1, 2), groups_of_two, 0)

    lane1 = lane[:1]
    summed = found[0:rows, 0, :]
    for part in range(1, 8):
        summed = summed + found[0:rows, part, :]
    summed = summed * (1.0 / VIEWS)
    for place in range(rows):
        block = lax.div(place, deep)
        base = block * deep + lax.rem(place - block * deep, pair_rate) + pair_rate
        row = summed[place : place + 1]
        turned = [
            pltpu.roll(row[:, t * LANES : (t + 1) * LANES], lax.rem(LANES - base, LANES), 1)
            for t in range(tiles)
        ]
        out[place : place + 1, :] = jnp.concatenate(
            [
                jnp.where(lane1 < LANES - base, turned[t], turned[(t + 1) % tiles])
                for t in range(tiles)
            ],
            1,
        )


def weights_kernel(
    conv_weight,
    pair_left,
    pair_right,
    pair_weight,
    pair_bias,
    head,
    conv_bias,
    shifts,
    flags,
    dilations,
    conv,
    project,
    pair,
    floor,
    out_head,
    out_bias,
    out_numbers,
    ones,
    wide,
):
    row = lax.broadcasted_iota(jnp.int32, (CHANNELS, CHANNELS), 0)
    column = lax.broadcasted_iota(jnp.int32, (CHANNELS, CHANNELS), 1)
    turn = (row + column == CHANNELS - 1).astype(jnp.float32).astype(jnp.bfloat16)
    for tap in range(3):
        here = slice(tap * CHANNELS, (tap + 1) * CHANNELS)
        there = slice((2 - tap) * CHANNELS, (3 - tap) * CHANNELS)
        conv[here, 0:CHANNELS] = conv_weight[here, :]
        conv[here, CHANNELS:] = jnp.dot(
            turn, conv_weight[there, :], preferred_element_type=jnp.float32
        ).astype(jnp.bfloat16)
    project[0:PAIR_CH, :] = pair_left[...]
    project[PAIR_CH:, :] = pair_right[...]
    taps = 9 * PAIR_CH
    wide[...] = jnp.zeros(wide.shape, jnp.float32)
    turned = pair_weight[...].astype(jnp.float32).T
    for half in range(PACK):
        start = half * (taps // 3)
        wide[half * PAIR_CH : (half + 1) * PAIR_CH, start : start + taps] = turned
    pair[...] = wide[...].astype(jnp.bfloat16)
    floor[...] = -jnp.broadcast_to(pair_bias[...], (LANES, PAIR_CH)).T
    out_bias[...] = conv_bias[...]
    out_numbers[:, 0:VIEWS] = shifts[...]
    out_numbers[:, VIEWS : 2 * VIEWS] = flags[...]
    out_numbers[:, 2 * VIEWS :] = dilations[...]
    row = lax.broadcasted_iota(jnp.int32, ones.shape, 0)
    column = lax.broadcasted_iota(jnp.int32, ones.shape, 1)
    ones[...] = (lax.rem(row, SPREAD) == lax.div(column, LANES)).astype(jnp.float32).astype(jnp.bfloat16)
    out_head[...] = jnp.broadcast_to(head[...].astype(jnp.float32), (LANES, PAIR_CH)).T


def prepared(
    reach,
    conv_weight,
    pair_left,
    pair_right,
    pair_weight,
    pair_bias,
    head,
    conv_bias,
    shifts,
    flags,
    dilations,
):
    whole = pl.BlockSpec(memory_space=pltpu.VMEM)
    made = [
        ((3 * CHANNELS, 2 * CHANNELS), jnp.bfloat16),
        ((2 * PAIR_CH, CHANNELS), jnp.bfloat16),
        ((PACK * PAIR_CH, 3 * CELLS * PAIR_CH), jnp.bfloat16),
        ((PAIR_CH, LANES), jnp.float32),
        ((PAIR_CH, LANES), jnp.float32),
        ((1, CHANNELS), jnp.float32),
        ((1, 2 * VIEWS + 2), jnp.int32),
        ((2 * SPREAD, reach * LANES), jnp.bfloat16),
    ]
    return pl.pallas_call(
        weights_kernel,
        out_shape=[pltpu.VMEM(*one) for one in made],
        in_specs=[whole] * 10,
        out_specs=[whole] * 8,
        scratch_shapes=[pltpu.VMEM((PACK * PAIR_CH, 3 * CELLS * PAIR_CH), jnp.float32)],
        cost_estimate=pl.CostEstimate(flops=10**9, bytes_accessed=10**6, transcendentals=0),
    )(
        conv_weight.reshape(3 * CHANNELS, CHANNELS),
        pair_left.T,
        pair_right.T,
        pair_weight.reshape(9 * PAIR_CH, PAIR_CH),
        pair_bias[None],
        head[None],
        conv_bias[None],
        shifts[None],
        flags[None],
        dilations[None],
    )


def main_call(rows, total, near, far, across_far, weights):
    span = -(-(BAND + rows + 2 * EDGE) // 16) * 16
    width = -(-span // LANES) * LANES
    whole = pl.BlockSpec(memory_space=pltpu.VMEM)
    return pl.pallas_call(
        functools.partial(kernel, rows, total),
        out_shape=jax.ShapeDtypeStruct((rows, BAND), jnp.float32),
        in_specs=[whole] * 11,
        out_specs=whole,
        scratch_shapes=[
            pltpu.VMEM((total + span + EDGE, CHANNELS), jnp.float32),
            pltpu.VMEM((2, 2 * PAIR_CH, width), jnp.bfloat16),
            pltpu.VMEM((VIEWS, rows + 3 * DMAX, PAIR_CH, LANES), jnp.bfloat16),
            pltpu.VMEM((VIEWS, STEPS + 1, PAIR_CH, width), jnp.bfloat16),
            pltpu.VMEM((VIEWS, rows + 2 * DMAX, PAIR_CH, LANES), jnp.float32),
            pltpu.VMEM((rows + 2 * DMAX, 8, BAND), jnp.float32),
        ],
        compiler_params=pltpu.CompilerParams(vmem_limit_bytes=40 << 20),
    )(near, far, across_far, *weights)


def per_device(
    bins,
    conv_weight,
    conv_bias,
    pair_left,
    pair_right,
    pair_weight,
    pair_bias,
    head,
    shifts,
    flags,
    dilations,
):
    rows = bins.shape[0]
    segments = lax.axis_size("seg")

    def exchanged(value, masks):
        route = [(i, i ^ masks[i % 2]) for i in range(segments)]
        return lax.ppermute(value, "seg", route)

    near = jnp.concatenate([bins, exchanged(bins, (1, 1))], 0)
    parts = [exchanged(near, (2 * even, 2 * odd)) for even, odd in rounds(segments)]
    weights = prepared(
        rows + 3 * DMAX,
        conv_weight,
        pair_left,
        pair_right,
        pair_weight,
        pair_bias,
        head,
        conv_bias,
        shifts,
        flags,
        dilations,
    )
    parts, weights = lax.optimization_barrier((parts, weights))
    far = jnp.concatenate(parts, 0)
    across_far = exchanged(far, (1, 1))
    return main_call(rows, rows * segments, near, far, across_far, weights)


def solution(mesh):
    placed = (P(("groups", "seg"), None), P(), P(), P(), P(), P(), P(), P(), P(), P(), P())
    return jax.shard_map(
        per_device,
        mesh=mesh,
        in_specs=placed,
        out_specs=P(("groups", "seg"), None),
        check_vma=False,
    )
```

```python
import functools

import jax
import jax.numpy as jnp
from jax import lax
from jax.experimental import pallas as pl
from jax.experimental.pallas import tpu as pltpu
from jax.sharding import PartitionSpec as P

CHANNELS = 128
PAIR_CH = 48
BAND = 512
VIEWS = 4
DMAX = 4
HALO = 20
EDGE = DMAX + HALO
LANES = 128
OUT = -1e30
PACK = 3
TOGETHER = 4
SPREAD = 64
CELLS = PACK + 2
STEPS = PACK + 4


def rounds(segments):
    chips = segments // 2
    return [(max(m, 1), m + 1) for m in range(0, chips, 2)]


def taken(tiles, amount):
    lane = lax.broadcasted_iota(jnp.int32, tiles[0].shape, 1)
    turned = [pltpu.roll(tile, (LANES - amount) % LANES, 1) for tile in tiles]
    keep = lane < LANES - amount
    return [
        jnp.where(keep, turned[t], turned[min(t + 1, len(tiles) - 1)]) for t in range(len(tiles))
    ]


def kernel(
    rows,
    total,
    *refs,
):
    (near, far, across_far, conv, project, pair, floor, head, conv_bias, numbers, ones) = refs[:11]
    (out, padded, sides, lefts, rights, floors, found) = refs[11:18]
    shifts = [numbers[0, place] for place in range(VIEWS)]
    flags = [numbers[0, VIEWS + place] for place in range(VIEWS)]
    dilations = [numbers[0, 2 * VIEWS + place] for place in range(2)]
    reach = rows + 3 * DMAX
    span = -(-(BAND + rows + 2 * EDGE) // 16) * 16
    first = lax.axis_index("seg") * rows
    seq_rate = dilations[0]
    pair_rate = dilations[1]

    padded[0:EDGE, :] = jnp.zeros((EDGE, CHANNELS), jnp.float32)
    padded[EDGE + total :, :] = jnp.zeros(
        (padded.shape[0] - EDGE - total, CHANNELS), jnp.float32
    )
    me = lax.div(first, rows)
    pieces = [(near, 0, me)]
    for turn, masks in enumerate(rounds(total // rows)):
        even = lax.rem(me, 2) == 0
        ours = jnp.where(even, masks[0], masks[1])
        theirs = jnp.where(even, masks[1], masks[0])
        pieces.append((far, 2 * rows * turn, lax.bitwise_xor(me, 2 * ours)))
        pieces.append(
            (across_far, 2 * rows * turn, lax.bitwise_xor(lax.bitwise_xor(me, 1), 2 * theirs))
        )
    for ref, start, segment in pieces:
        for core in range(2):
            place = lax.bitwise_xor(segment, core) * rows
            padded[pl.ds(pl.multiple_of(EDGE + place, 8), rows), :] = ref[
                start + core * rows : start + (core + 1) * rows, :
            ].astype(jnp.float32)
    taps = [
        padded[pl.ds(first + DMAX + (tap - 1) * seq_rate, span), :] for tap in range(3)
    ]
    stacked = jnp.concatenate([tap.astype(jnp.bfloat16) for tap in taps], 1)
    mixed = jnp.dot(stacked, conv[...], preferred_element_type=jnp.float32)
    for flag in range(2):
        part = mixed[:, flag * CHANNELS : (flag + 1) * CHANNELS]
        feature = (taps[1] + jnp.maximum(part + conv_bias[...], 0.0)).astype(jnp.bfloat16)
        both = lax.dot_general(
            project[...], feature, (((1,), (1,)), ((), ())), preferred_element_type=jnp.float32
        )
        sides[flag, :, span:] = jnp.zeros((2 * PAIR_CH, sides.shape[2] - span), jnp.bfloat16)
        sides[flag, :, 0:span] = both.astype(jnp.bfloat16)

    width = sides.shape[2]
    tiles = BAND // LANES
    lane = lax.broadcasted_iota(jnp.int32, (PAIR_CH, LANES), 1)

    def prepare(view):
        shift = shifts[view]
        flag = flags[view]
        both = sides[flag]
        cut = [both[:, t * LANES : (t + 1) * LANES] for t in range(width // LANES)]
        left = taken([c[:PAIR_CH] for c in cut[:2]], shift + HALO - DMAX)[0]
        place = first - DMAX + lane
        left = jnp.where((place >= 0) & (place < total), left, 0.0).astype(jnp.bfloat16)
        turned = [left] + [pltpu.roll(left, LANES - by * pair_rate, 1) for by in (1, 2)]
        level = [
            pltpu.roll(value, (LANES + pair_rate - DMAX) % LANES, 1)
            for value in turned
        ]
        spread = jnp.concatenate([value for value in level for _ in range(3)], 0)
        low = floor[...] - jnp.dot(
            pair[0:PAIR_CH, 0 : 9 * PAIR_CH], spread, preferred_element_type=jnp.float32
        )
        high = low.astype(jnp.bfloat16)
        rest = (low - high.astype(jnp.float32)).astype(jnp.bfloat16)
        lows_of.append(jnp.concatenate([high[:, 0:SPREAD], rest[:, 0:SPREAD]], 1))
        rows_of.append(-left[:, 0:SPREAD])
        rights[view, STEPS] = jnp.full((PAIR_CH, width), OUT, jnp.bfloat16)
        for step in range(STEPS):
            offset = (step - 3) * pair_rate
            right = taken([c[PAIR_CH:] for c in cut], shift + HALO + offset)
            for t in range(width // LANES):
                rights[view, step, :, t * LANES : (t + 1) * LANES] = jnp.where(
                    first + offset + t * LANES + lane < total, right[t], OUT
                ).astype(jnp.bfloat16)

    rows_of = []
    lows_of = []
    for view in range(VIEWS):
        prepare(view)
    stacked = jnp.concatenate(rows_of, 0)
    for row in range(0, reach, 4):
        spread = jnp.dot(
            stacked,
            ones[0:SPREAD, row * LANES : (row + 4) * LANES],
            preferred_element_type=jnp.float32
        ).astype(jnp.bfloat16)
        for view in range(VIEWS):
            for which in range(4):
                lefts[view, row + which] = spread[
                    view * PAIR_CH : (view + 1) * PAIR_CH, which * LANES : (which + 1) * LANES
                ]

    stacked = jnp.concatenate(lows_of, 0)
    for row in range(0, rows + 2 * DMAX, 4):
        spread = jnp.dot(
            stacked, ones[:, row * LANES : (row + 4) * LANES], preferred_element_type=jnp.float32
        )
        for view in range(VIEWS):
            for which in range(4):
                floors[view, row + which] = spread[
                    view * PAIR_CH : (view + 1) * PAIR_CH, which * LANES : (which + 1) * LANES
                ]

    def group(number):
        block = lax.div(number, pair_rate)
        base = number + block * (PACK - 1) * pair_rate
        sums = [[0.0] * tiles for _ in range(PACK)]
        offsets = [0.0] * PACK
        seam = base + pair_rate
        wrapped = lane < seam
        caps = [
            jnp.where(gone, OUT, -OUT).astype(jnp.bfloat16)
            for gone in (
                (lane >= seam) & (lane < seam + pair_rate),
                (lane >= base) & (lane < seam),
            )
        ]
        for view in range(VIEWS):
            sides_of = [
                lefts[view, base + DMAX + (cell - 1) * pair_rate] for cell in range(CELLS)
            ]
            above = first + base < pair_rate
            lows = []
            for half in range(PACK):
                lows.append(floors[view, base + half * pair_rate])
                for e in range(0, PAIR_CH, 8):
                    offsets[half] = offsets[half] + lows[half][e : e + 8] * head[e : e + 8, :]
            for wide in range(tiles // 2):
                chosen = (2 * wide, 2 * wide + 1)
                across = {}
                for step in range(-3, STEPS):
                    at = step if step >= 0 else jnp.where(above, STEPS, step + 3)
                    row = [rights[view, at, :, t * LANES : (t + 1) * LANES] for t in chosen]
                    if wide == 0:
                        last = rights[view, at, :, tiles * LANES :]
                        row[0] = jnp.where(wrapped, last, row[0])
                    across[step] = row
                cells = []
                for cell in range(CELLS):
                    for tap in range(3):
                        row = list(across[cell + tap if cell else tap - 3])
                        if wide == 0 and tap == 0:
                            row[0] = jnp.minimum(row[0], caps[0])
                        if wide == 0 and tap == 2:
                            row[0] = jnp.minimum(row[0], caps[1])
                        cells.append(
                            jnp.concatenate([jnp.maximum(r, sides_of[cell]) for r in row], 1)
                        )
                stack = jnp.concatenate(cells, 0)
                product = jnp.dot(pair[...], stack, preferred_element_type=jnp.float32)
                for half in range(PACK):
                    for t in chosen:
                        for e in range(0, PAIR_CH, 8):
                            part = product[
                                half * PAIR_CH + e : half * PAIR_CH + e + 8,
                                (t - chosen[0]) * LANES : (t - chosen[0] + 1) * LANES,
                            ]
                            sums[half][t] = (
                                sums[half][t]
                                + jnp.maximum(part, lows[half][e : e + 8]) * head[e : e + 8, :]
                            )
        sums = [[sums[half][t] - offsets[half] for t in range(tiles)] for half in range(PACK)]
        for half in range(PACK):
            found[base + half * pair_rate] = jnp.concatenate(sums[half], 1)

    def some_groups(number, carry):
        for which in range(TOGETHER):
            group(TOGETHER * number + which)
        return carry

    deep = PACK * pair_rate
    groups = lax.div(rows + deep - 1, deep) * pair_rate
    lax.fori_loop(0, lax.div(groups + TOGETHER - 1, TOGETHER), some_groups, 0)

    lane1 = lane[:1]
    summed = found[0:rows, 0, :]
    for part in range(1, 8):
        summed = summed + found[0:rows, part, :]
    summed = summed * (1.0 / VIEWS)
    for place in range(rows):
        block = lax.div(place, deep)
        base = block * deep + lax.rem(place - block * deep, pair_rate) + pair_rate
        row = summed[place : place + 1]
        turned = [
            pltpu.roll(row[:, t * LANES : (t + 1) * LANES], lax.rem(LANES - base, LANES), 1)
            for t in range(tiles)
        ]
        out[place : place + 1, :] = jnp.concatenate(
            [
                jnp.where(lane1 < LANES - base, turned[t], turned[(t + 1) % tiles])
                for t in range(tiles)
            ],
            1,
        )


def weights_kernel(
    conv_weight,
    pair_left,
    pair_right,
    pair_weight,
    pair_bias,
    head,
    conv_bias,
    shifts,
    flags,
    dilations,
    conv,
    project,
    pair,
    floor,
    out_head,
    out_bias,
    out_numbers,
    ones,
    wide,
):
    row = lax.broadcasted_iota(jnp.int32, (CHANNELS, CHANNELS), 0)
    column = lax.broadcasted_iota(jnp.int32, (CHANNELS, CHANNELS), 1)
    turn = (row + column == CHANNELS - 1).astype(jnp.float32).astype(jnp.bfloat16)
    for tap in range(3):
        here = slice(tap * CHANNELS, (tap + 1) * CHANNELS)
        there = slice((2 - tap) * CHANNELS, (3 - tap) * CHANNELS)
        conv[here, 0:CHANNELS] = conv_weight[here, :]
        conv[here, CHANNELS:] = jnp.dot(
            turn, conv_weight[there, :], preferred_element_type=jnp.float32
        ).astype(jnp.bfloat16)
    project[0:PAIR_CH, :] = pair_left[...]
    project[PAIR_CH:, :] = pair_right[...]
    taps = 9 * PAIR_CH
    wide[...] = jnp.zeros(wide.shape, jnp.float32)
    turned = pair_weight[...].astype(jnp.float32).T
    for half in range(PACK):
        start = half * (taps // 3)
        wide[half * PAIR_CH : (half + 1) * PAIR_CH, start : start + taps] = turned
    pair[...] = wide[...].astype(jnp.bfloat16)
    floor[...] = -jnp.broadcast_to(pair_bias[...], (LANES, PAIR_CH)).T
    out_bias[...] = conv_bias[...]
    out_numbers[:, 0:VIEWS] = shifts[...]
    out_numbers[:, VIEWS : 2 * VIEWS] = flags[...]
    out_numbers[:, 2 * VIEWS :] = dilations[...]
    row = lax.broadcasted_iota(jnp.int32, ones.shape, 0)
    column = lax.broadcasted_iota(jnp.int32, ones.shape, 1)
    ones[...] = (lax.rem(row, SPREAD) == lax.div(column, LANES)).astype(jnp.float32).astype(jnp.bfloat16)
    out_head[...] = jnp.broadcast_to(head[...].astype(jnp.float32), (LANES, PAIR_CH)).T


def prepared(
    reach,
    conv_weight,
    pair_left,
    pair_right,
    pair_weight,
    pair_bias,
    head,
    conv_bias,
    shifts,
    flags,
    dilations,
):
    whole = pl.BlockSpec(memory_space=pltpu.VMEM)
    made = [
        ((3 * CHANNELS, 2 * CHANNELS), jnp.bfloat16),
        ((2 * PAIR_CH, CHANNELS), jnp.bfloat16),
        ((PACK * PAIR_CH, 3 * CELLS * PAIR_CH), jnp.bfloat16),
        ((PAIR_CH, LANES), jnp.float32),
        ((PAIR_CH, LANES), jnp.float32),
        ((1, CHANNELS), jnp.float32),
        ((1, 2 * VIEWS + 2), jnp.int32),
        ((2 * SPREAD, reach * LANES), jnp.bfloat16),
    ]
    return pl.pallas_call(
        weights_kernel,
        out_shape=[pltpu.VMEM(*one) for one in made],
        in_specs=[whole] * 10,
        out_specs=[whole] * 8,
        scratch_shapes=[pltpu.VMEM((PACK * PAIR_CH, 3 * CELLS * PAIR_CH), jnp.float32)],
        cost_estimate=pl.CostEstimate(flops=10**9, bytes_accessed=10**6, transcendentals=0),
    )(
        conv_weight.reshape(3 * CHANNELS, CHANNELS),
        pair_left.T,
        pair_right.T,
        pair_weight.reshape(9 * PAIR_CH, PAIR_CH),
        pair_bias[None],
        head[None],
        conv_bias[None],
        shifts[None],
        flags[None],
        dilations[None],
    )


def main_call(rows, total, near, far, across_far, weights):
    span = -(-(BAND + rows + 2 * EDGE) // 16) * 16
    width = -(-span // LANES) * LANES
    whole = pl.BlockSpec(memory_space=pltpu.VMEM)
    return pl.pallas_call(
        functools.partial(kernel, rows, total),
        out_shape=jax.ShapeDtypeStruct((rows, BAND), jnp.float32),
        in_specs=[whole] * 11,
        out_specs=whole,
        scratch_shapes=[
            pltpu.VMEM((total + span + EDGE, CHANNELS), jnp.float32),
            pltpu.VMEM((2, 2 * PAIR_CH, width), jnp.bfloat16),
            pltpu.VMEM((VIEWS, rows + 3 * DMAX, PAIR_CH, LANES), jnp.bfloat16),
            pltpu.VMEM((VIEWS, STEPS + 1, PAIR_CH, width), jnp.bfloat16),
            pltpu.VMEM((VIEWS, rows + 2 * DMAX, PAIR_CH, LANES), jnp.float32),
            pltpu.VMEM((rows + 2 * DMAX, 8, BAND), jnp.float32),
        ],
        compiler_params=pltpu.CompilerParams(vmem_limit_bytes=40 << 20),
    )(near, far, across_far, *weights)


def per_device(
    bins,
    conv_weight,
    conv_bias,
    pair_left,
    pair_right,
    pair_weight,
    pair_bias,
    head,
    shifts,
    flags,
    dilations,
):
    rows = bins.shape[0]
    segments = lax.axis_size("seg")

    def exchanged(value, masks):
        route = [(i, i ^ masks[i % 2]) for i in range(segments)]
        return lax.ppermute(value, "seg", route)

    near = jnp.concatenate([bins, exchanged(bins, (1, 1))], 0)
    parts = [exchanged(near, (2 * even, 2 * odd)) for even, odd in rounds(segments)]
    weights = prepared(
        rows + 3 * DMAX,
        conv_weight,
        pair_left,
        pair_right,
        pair_weight,
        pair_bias,
        head,
        conv_bias,
        shifts,
        flags,
        dilations,
    )
    parts, weights = lax.optimization_barrier((parts, weights))
    far = jnp.concatenate(parts, 0)
    across_far = exchanged(far, (1, 1))
    return main_call(rows, rows * segments, near, far, across_far, weights)


def solution(mesh):
    placed = (P(("groups", "seg"), None), P(), P(), P(), P(), P(), P(), P(), P(), P(), P())
    return jax.shard_map(
        per_device,
        mesh=mesh,
        in_specs=placed,
        out_specs=P(("groups", "seg"), None),
        check_vma=False,
    )
```
